512 devices in a mesh: rows: 32 (over z, core), feat: 16 (over y, x).
Axes of the slice: x: 4, y: 4, z: 16, core: 2. Of those that a mesh axis runs over, the one named last changes fastest.
Arguments:
- features: bfloat16 [163840, 8192], P('rows', 'feat'), may hold values from -0.015625 to 0.015625
- targets: float32 [163840], P('rows'), may hold values from -6 to 6
- target_noise: float32 [96, 163840], P(None, 'rows'), may hold values from -6 to 6
- prior_noise: float32 [96, 8192], P(None, 'feat'), may hold values from -6 to 6
- precision: float32 [8192], P('feat'), may hold values from 0.5 to 2
Outputs:
- sampled_coefficients: float32 [96, 8192], P(None, 'feat')
- residual: float32 [96, 8192], P(None, 'feat')
The draws below stay inside these ranges and needn't reach their ends.
All inputs are finite; a program needn't handle non-finite values.
Results may differ from the reference program's by a relative error of at most 0.025.
Values may be sent and summed in bfloat16 or wider, within the bound.
No kernel may reach another device: no remote copies, remote signals or barrier semaphores. Data moves between devices by JAX's collectives and lax.ppermute only.
A program may use at most 64 MiB of HBM per device.

```python
import math
import jax
import jax.numpy as jnp
from jax import lax

D = 8192
ROWS_DEV = 5120
DRAWS = 96
ITERS = 2
ROWS = 163840
N_ROWS = 32


def block_levels(stream_key, shape, cuts, low, largest):
    def one(position, blocks):
        steps = jax.random.uniform(jax.random.fold_in(jax.random.fold_in(stream_key, 6), position), (blocks,), jnp.float32, low / len(cuts), largest / len(cuts))
        return jnp.repeat(jnp.exp(steps), shape[position] // blocks).reshape((-1,) + (1,) * (len(shape) - position - 1))

    level = one(*cuts[0])
    for cut in cuts[1:]:
        level = level * one(*cut)
    return level


def bell_draw(stream_key, dims, spread, bound, pieces=(), kind=jnp.bfloat16):
    values = jax.random.normal(stream_key, dims, jnp.float32) * spread
    if len(pieces) > 0:
        values = block_levels(stream_key, dims, pieces, -0.22, 0.18) * values
    return jnp.clip(values, min=-bound, max=bound).astype(kind)


def setup_inputs(seed: int = 0) -> dict:
    seeds = jax.random.split(jax.random.key(seed), 6)
    features = bell_draw(seeds[0], (ROWS, D), ROWS ** -0.5, 0.015625, ((0, 32), (1, 16)))
    targets = bell_draw(seeds[1], (ROWS,), 1.0, 6.0, ((0, 32),), jnp.float32)
    target_noise = bell_draw(seeds[2], (DRAWS, ROWS), 1.0, 6.0, ((1, 32),), jnp.float32)
    prior_noise = bell_draw(seeds[3], (DRAWS, D), 1.0, 6.0, ((1, 16),), jnp.float32)
    precision = jnp.clip(jnp.exp(math.log(2.0) - 1.3862944 * jax.random.uniform(seeds[4], (D,), jnp.float32) ** block_levels(seeds[4], (D,), ((0, 16),), -0.2, 0.2)), 0.5, 2.0)
    return dict(features=features, targets=targets, target_noise=target_noise, prior_noise=prior_noise, precision=precision)


def reference(features, targets, target_noise, prior_noise, precision):
    block_list = features.reshape(N_ROWS, ROWS_DEV, D)
    perturbed_targets = targets[None, :] + target_noise

    def image(direction):
        piece = direction.astype(jnp.bfloat16).astype(jnp.float32)

        def one_block(block_slice):
            return jnp.einsum('sd,rd->sr', piece, block_slice.astype(jnp.float32), precision=lax.Precision.HIGHEST)
        out = lax.map(one_block, block_list)
        return jnp.transpose(out, (1, 0, 2)).reshape(DRAWS, ROWS)

    def back(error_terms):
        high = error_terms.astype(jnp.bfloat16)
        low = (error_terms - high.astype(jnp.float32)).astype(jnp.bfloat16)
        high_blocks = jnp.transpose(high.astype(jnp.float32).reshape(DRAWS, N_ROWS, ROWS_DEV), (1, 0, 2))
        low_blocks = jnp.transpose(low.astype(jnp.float32).reshape(DRAWS, N_ROWS, ROWS_DEV), (1, 0, 2))

        def add_block(total, triple):
            block_slice, high_err, low_err = triple
            wide = block_slice.astype(jnp.float32)
            term = jnp.einsum('sr,rk->sk', high_err, wide, precision=lax.Precision.HIGHEST)
            term = term + jnp.einsum('sr,rk->sk', low_err, wide, precision=lax.Precision.HIGHEST)
            return (total + term, None)
        total, _ = lax.scan(add_block, jnp.zeros((DRAWS, D), jnp.float32), (block_list, high_blocks, low_blocks))
        return total
    prior_sample = prior_noise * lax.rsqrt(precision)[None, :]
    fitted = image(prior_sample)
    error_terms = perturbed_targets - fitted
    residual = back(error_terms)
    direction = residual
    solution = prior_sample
    norm_now = lax.optimization_barrier(jnp.sum(residual * residual, axis=1))
    for step in range(ITERS):
        operator_result = back(image(direction)) + precision[None, :] * direction
        alpha = norm_now / lax.optimization_barrier(jnp.sum(direction * operator_result, axis=1))
        solution = solution + alpha[:, None] * direction
        residual = residual - alpha[:, None] * operator_result
        norm_next = lax.optimization_barrier(jnp.sum(residual * residual, axis=1))
        direction = residual + (norm_next / norm_now)[:, None] * direction
        norm_now = norm_next
    return (solution, residual)
```

```python
import functools
import math

import jax
import jax.numpy as jnp
from jax import lax
from jax.experimental import pallas as pl
from jax.experimental.pallas import tpu as pltpu
from jax.sharding import PartitionSpec as P

CORES = 2
LANES = 128
BLOCKS = 4
F32, BF16 = jnp.float32, jnp.bfloat16
MOST = 16 * 2**20
WHOLE = 56 * 2**20
SCALARS = 16
LITTLE = 8 * 2**20
IN_VMEM = pl.BlockSpec(memory_space=pltpu.VMEM)
SMALL = pl.CostEstimate(flops=2**16, bytes_accessed=2**22, transcendentals=0)


def lane_index(rows):
    return lax.broadcasted_iota(jnp.int32, (rows, LANES), 1)


def column_to_row(column):
    rows = column.shape[0]
    at = lax.broadcasted_iota(jnp.int32, (rows, LANES), 0) == lane_index(rows)
    return jnp.sum(jnp.where(at, column, 0.0), axis=0, keepdims=True)


def row_to_column(row, rows, first=0):
    at = lax.broadcasted_iota(jnp.int32, (rows, LANES), 0) + first == lane_index(rows)
    return jnp.sum(jnp.where(at, row, 0.0), axis=1, keepdims=True)


def split(value):
    high = value.astype(BF16).astype(F32)
    return high, value - high


def assemble(pieces_ref, whole):
    tall = pieces_ref.shape[1]
    across = whole.shape[1] // LANES
    for m in range(pieces_ref.shape[0]):
        i, j = divmod(m, across)
        whole[pl.ds(i * tall, tall), pl.ds(j * LANES, LANES)] = pieces_ref[m].astype(F32)


def multiply_out(value, f_ref, store, wide, copies=None):
    chunks = f_ref.shape[0] // wide
    blocks = math.gcd(chunks, BLOCKS)
    per = chunks // blocks
    size = per * wide
    for k in range(blocks):
        if copies is not None:
            copies[k].wait()
        terms = lax.dot_general(
            value,
            f_ref[pl.ds(k * size, size)],
            (((1,), (1,)), ((), ())),
            preferred_element_type=F32,
        )
        for c in range(per):
            store(k * per + c, terms[:, c * wide : (c + 1) * wide])


def fetch(f_hbm, kept_ref, sems):
    count = sems.shape[0]
    size = f_hbm.shape[0] // count
    copies = []
    for k in range(count):
        at = pl.ds(k * size, size)
        copies.append(pltpu.make_async_copy(f_hbm.at[at], kept_ref.at[at], sems.at[k]))
        copies[k].start()
    return copies


def multiply_into(value, f_ref, pieces_ref, first, copies=None):
    def store(c, part):
        pieces_ref[first + c] = part.astype(BF16)

    multiply_out(value, f_ref, store, pieces_ref.shape[2], copies)


def own_image_kernel(
    core_ref, noise_ref, scale_ref, own_hbm, pieces_ref, value_ref, kept_ref, sems
):
    copies = fetch(own_hbm, kept_ref, sems)
    draws = pieces_ref.shape[1]
    first = pl.multiple_of(core_ref[0] * draws, 8)
    value = (noise_ref[pl.ds(first, draws)] * lax.rsqrt(scale_ref[...])).astype(BF16)
    value_ref[...] = value
    multiply_into(value, kept_ref, pieces_ref, 0, copies)


def other_image_kernel(value_ref, half_ref, other_hbm, pieces_ref, kept_ref, sems):
    copies = fetch(other_hbm, kept_ref, sems)
    count = half_ref.shape[0]
    for c in range(count):
        pieces_ref[c] = half_ref[c]
    multiply_into(value_ref[...], kept_ref, pieces_ref, count, copies)


def image_kernel(count, scale_ref, own_ref, other_ref, *refs):
    vectors, (pieces_ref, sums_ref), wholes = (
        refs[:count],
        refs[count : count + 2],
        refs[count + 2 :],
    )
    for source, whole in zip(vectors, wholes):
        assemble(source, whole)
    value = wholes[0][...]
    direction = value.astype(BF16)
    multiply_into(direction, own_ref, pieces_ref, 0)
    multiply_into(direction, other_ref, pieces_ref, pieces_ref.shape[0] // CORES)
    sums = [value * value, value * value * scale_ref[...]]
    if count > 1:
        sums.append(value * wholes[1][...])
    lines = []
    for product in sums:
        column = jnp.sum(product, axis=1, keepdims=True)
        lines += [column_to_row(part) for part in split(column)]
    lines.append(jnp.zeros((SCALARS - len(lines), LANES), F32))
    sums_ref[...] = jnp.concatenate(lines, axis=0).astype(BF16)


def matmul_cost(draws, rows, width):
    return pl.CostEstimate(
        flops=2 * draws * rows * width, bytes_accessed=2 * rows * width, transcendentals=0
    )


def first_image_terms(core, noise, scale, own, other, n_feat):
    rows, width = own.shape
    draws = noise.shape[0] // CORES
    shape = (n_feat // CORES, draws, CORES * rows // n_feat)
    anywhere = [pl.BlockSpec(memory_space=pl.ANY)]
    kept = jax.ShapeDtypeStruct((rows, width), BF16)
    sems = [pltpu.SemaphoreType.DMA((math.gcd(shape[0], BLOCKS),))]
    params = pltpu.CompilerParams(vmem_limit_bytes=WHOLE)
    half, value = pl.pallas_call(
        own_image_kernel,
        in_specs=[pl.BlockSpec(memory_space=pltpu.SMEM)] + [IN_VMEM] * 2 + anywhere,
        out_specs=[IN_VMEM] * 2,
        out_shape=[
            jax.ShapeDtypeStruct(shape, BF16),
            jax.ShapeDtypeStruct((draws, width), BF16),
        ],
        scratch_shapes=[pltpu.VMEM((rows, width), BF16)] + sems,
        compiler_params=params,
        cost_estimate=matmul_cost(draws, rows, width),
    )(core, noise, scale, own)
    params = pltpu.CompilerParams(vmem_limit_bytes=MOST)
    terms, other = pl.pallas_call(
        other_image_kernel,
        in_specs=[IN_VMEM] * 2 + anywhere,
        out_specs=[IN_VMEM] * 2,
        out_shape=[jax.ShapeDtypeStruct((n_feat,) + shape[1:], BF16), kept],
        scratch_shapes=sems,
        compiler_params=params,
        cost_estimate=matmul_cost(draws, rows, width),
    )(value, half, other)
    return terms, other


def image_terms(scale, own, other, vectors, n_feat):
    rows, width = own.shape
    draws = vectors[0].size // width
    count = len(vectors)
    return pl.pallas_call(
        functools.partial(image_kernel, count),
        in_specs=[IN_VMEM] * (3 + count),
        out_specs=[IN_VMEM] * 2,
        out_shape=[
            jax.ShapeDtypeStruct((n_feat, draws, CORES * rows // n_feat), BF16),
            jax.ShapeDtypeStruct((SCALARS, LANES), BF16),
        ],
        scratch_shapes=[pltpu.VMEM((draws, width), F32)] * count,
        compiler_params=pltpu.CompilerParams(vmem_limit_bytes=MOST),
        cost_estimate=matmul_cost(draws, CORES * rows, width),
    )(scale, own, other, *vectors)


def sum_kernel(first, terms_ref, more_ref, message_ref):
    count, tall, wide = terms_ref.shape
    total = terms_ref[0].astype(F32)
    for k in range(1, count):
        total = total + terms_ref[k].astype(F32)
    if first:
        total = more_ref[...] - total
    total = total.astype(BF16)
    for k in range(count):
        for b in range(wide // LANES):
            at = pl.ds(b * tall, tall)
            message_ref[k, at] = total[:, b * LANES : (b + 1) * LANES]
        if not first:
            message_ref[k, pl.ds(wide // LANES * tall, SCALARS)] = more_ref[...]


def sum_terms(terms, more, first):
    count, tall, wide = terms.shape
    return pl.pallas_call(
        functools.partial(sum_kernel, first),
        out_shape=jax.ShapeDtypeStruct(
            (count, tall * wide // LANES + (0 if first else SCALARS), LANES), BF16
        ),
        compiler_params=pltpu.CompilerParams(vmem_limit_bytes=LITTLE),
        cost_estimate=pl.CostEstimate(
            flops=terms.size, bytes_accessed=4 * terms.size, transcendentals=0
        ),
    )(terms, more)


def back_kernel(first, message_ref, own_ref, other_ref, pieces_ref, sums_ref, errors):
    count = message_ref.shape[0]
    draws, wide = errors.shape[0], errors.shape[1] // count
    rows = own_ref.shape[0]
    for c in range(count):
        for b in range(wide // LANES):
            errors[:, pl.ds(c * wide + b * LANES, LANES)] = message_ref[
                c, pl.ds(b * draws, draws)
            ]
    total = jnp.dot(errors[:, pl.ds(0, rows)], own_ref[...], preferred_element_type=F32)
    total = total + jnp.dot(
        errors[:, pl.ds(rows, rows)], other_ref[...], preferred_element_type=F32
    )
    across = own_ref.shape[1] // LANES
    short = sums_ref.shape[1]
    if first:
        sums_ref[...] = jnp.zeros(sums_ref.shape, F32)
        for m in range(pieces_ref.shape[0]):
            i, j = divmod(m, across)
            piece = total[i * short : (i + 1) * short, j * LANES : (j + 1) * LANES]
            pieces_ref[m] = piece.astype(BF16)
        return
    squares = jnp.zeros((draws, LANES), F32)
    for at in range(0, errors.shape[1], LANES):
        part = errors[:, pl.ds(at, LANES)].astype(F32)
        squares = squares + part * part
    high, low = split(jnp.sum(squares, axis=1, keepdims=True))
    packed = jnp.zeros((SCALARS, LANES), F32)
    for k in range(count):
        part = message_ref[k, pl.ds(wide // LANES * draws, SCALARS)]
        packed = packed + part.astype(F32)
    lane = lane_index(short)
    empty = jnp.zeros((pieces_ref.shape[1] - short - 2, LANES), F32)
    for i in range(sums_ref.shape[0]):
        mine = slice(i * short, (i + 1) * short)
        plain = jnp.zeros((short, LANES), F32)
        for k in range(3):
            line = packed[2 * k : 2 * k + 1] + packed[2 * k + 1 : 2 * k + 2]
            plain = jnp.where(lane == k, row_to_column(line, short, i * short), plain)
        sums_ref[i] = plain
        extra = [column_to_row(high[mine]), column_to_row(low[mine]), empty]
        for j in range(across):
            piece = total[mine, j * LANES : (j + 1) * LANES]
            pieces_ref[i * across + j] = jnp.concatenate([piece] + extra, axis=0).astype(BF16)


def back_terms(message, own, other, draws, pieces, first):
    rows, width = own.shape
    short = draws * width // LANES // pieces
    return pl.pallas_call(
        functools.partial(back_kernel, first),
        in_specs=[IN_VMEM] * 3,
        out_specs=[IN_VMEM] * 2,
        out_shape=[
            jax.ShapeDtypeStruct(
                (pieces, short if first else (short + 17) // 16 * 16, LANES), BF16
            ),
            jax.ShapeDtypeStruct((draws // short, short, LANES), F32),
        ],
        scratch_shapes=[pltpu.VMEM((draws, CORES * rows), BF16)],
        compiler_params=pltpu.CompilerParams(vmem_limit_bytes=MOST),
        cost_estimate=matmul_cost(draws, CORES * rows, width),
    )(message, own, other)


def pick(sums_ref, group_ref, rows):
    mine = sums_ref[group_ref[0]]
    lane = lane_index(rows)
    return [
        jnp.sum(jnp.where(lane == k, mine, 0.0), axis=1, keepdims=True) for k in range(3)
    ]


def add_up(terms_ref):
    total = terms_ref[0].astype(F32)
    for k in range(1, terms_ref.shape[0]):
        total = total + terms_ref[k].astype(F32)
    return total


def received(terms_ref, rows):
    total = add_up(terms_ref)
    norm = row_to_column(total[rows : rows + 1] + total[rows + 1 : rows + 2], rows)
    return total[:rows], norm


def to_all(message_ref, value):
    value = value.astype(BF16)
    for k in range(message_ref.shape[0]):
        message_ref[k] = value


def first_kernel(terms_ref, message_ref, r0_ref):
    r0 = add_up(terms_ref)
    r0_ref[...] = r0
    to_all(message_ref, r0)


def second_kernel(
    group_ref, terms_ref, sums_ref, scale_ref, r0_ref, message_ref, r1_ref, q0_ref, scalar_ref
):
    rows = r0_ref.shape[0]
    product, norm = received(terms_ref, rows)
    rr, weighted, _ = pick(sums_ref, group_ref, rows)
    curve = norm + weighted
    alpha = rr / curve
    q0 = product + scale_ref[...] * r0_ref[...]
    r1 = r0_ref[...] - alpha * q0
    r1_ref[...] = r1
    q0_ref[...] = q0
    scalar_ref[0] = jnp.broadcast_to(rr, (rows, LANES))
    scalar_ref[1] = jnp.broadcast_to(alpha, (rows, LANES))
    scalar_ref[2] = jnp.broadcast_to(curve, (rows, LANES))
    to_all(message_ref, r1)


def third_kernel(
    group_ref, terms_ref, sums_ref, scale_ref, r0_ref, r1_ref, q0_ref, scalar_ref, message_ref
):
    rows = r0_ref.shape[0]
    product, norm = received(terms_ref, rows)
    new, weighted, cross = pick(sums_ref, group_ref, rows)
    rr, alpha0, curve0 = (scalar_ref[k][:, :1] for k in range(3))
    beta = new / rr
    mixed = (cross - new) / alpha0
    curve = norm + weighted + 2.0 * beta * mixed + beta * beta * curve0
    alpha = new / curve
    r1 = r1_ref[...]
    applied = product + scale_ref[...] * r1 + beta * q0_ref[...]
    parts = [r1 - alpha * applied]
    for scalar in (alpha0 + alpha * beta, alpha):
        parts += [column_to_row(part) for part in split(scalar)]
    short = message_ref.shape[1] - rows - 4
    if short > 0:
        parts.append(jnp.zeros((short, LANES), F32))
    to_all(message_ref, jnp.concatenate(parts, axis=0))


def small_call(kernel, group, operands, outs):
    specs = [IN_VMEM] * len(operands)
    if group is not None:
        specs = [pl.BlockSpec(memory_space=pltpu.SMEM)] + specs
        operands = (group,) + operands
    return pl.pallas_call(
        kernel,
        in_specs=specs,
        out_specs=[IN_VMEM] * len(outs),
        out_shape=[jax.ShapeDtypeStruct(shape, kind) for shape, kind in outs],
        compiler_params=pltpu.CompilerParams(vmem_limit_bytes=LITTLE),
        cost_estimate=SMALL,
    )(*operands)


def last_kernel(core_ref, pieces_ref, whole0_ref, whole1_ref, noise_ref, scale_ref, out_ref):
    tall = whole0_ref.shape[1]
    draws = out_ref.shape[1]
    across = out_ref.shape[2] // LANES
    first = pl.multiple_of(core_ref[0] * draws, 8)
    out_ref[0] = noise_ref[pl.ds(first, draws)] * lax.rsqrt(scale_ref[...])
    for m in range(pieces_ref.shape[0]):
        i, j = divmod(m, across)
        at = (pl.ds(i * tall, tall), pl.ds(j * LANES, LANES))
        piece = pieces_ref[m].astype(F32)
        part0, part1 = (
            row_to_column(piece[k : k + 1] + piece[k + 1 : k + 2], tall)
            for k in (tall, tall + 2)
        )
        moved = part0 * whole0_ref[m].astype(F32) + part1 * whole1_ref[m].astype(F32)
        out_ref[(0,) + at] = out_ref[(0,) + at] + moved
        out_ref[(1,) + at] = piece[:tall]


def join_kernel(core_ref, own_ref, other_ref, sampled_ref, residual_ref):
    draws = own_ref.shape[1]
    for core, source in ((core_ref[0], own_ref), (1 - core_ref[0], other_ref)):
        at = pl.ds(pl.multiple_of(core * draws, 8), draws)
        sampled_ref[at] = source[0]
        residual_ref[at] = source[1]


def shards(features, targets, target_noise, prior_noise, precision):
    n_feat = lax.axis_size("feat")
    n_rows = lax.axis_size("rows")
    draws, width = prior_noise.shape
    rows = features.shape[0]
    half = draws // CORES
    chunks = n_feat // CORES
    wide = rows // chunks
    deep = n_rows // CORES
    across = width // LANES
    short = half * across // deep

    levels = [[CORES * z + core for z in range(deep)] for core in range(CORES)]
    swap = [(i, i ^ 1) for i in range(n_rows)]
    other = lax.ppermute(features, "rows", swap)

    scale = precision[None, :]
    line = lax.axis_index("rows").astype(jnp.int32)
    height = line // CORES
    core = (line % CORES).reshape(1)
    group = (height // across).reshape(1)
    place = lax.axis_index("feat")
    first_row = (place % chunks) * wide
    my_targets = lax.dynamic_slice(targets, (first_row,), (wide,))[None, :]
    kept, sent = (
        my_targets + lax.dynamic_slice(target_noise, (side * half, first_row), (half, wide))
        for side in (core[0], 1 - core[0])
    )
    perturbed = jnp.where(place < chunks, kept, lax.ppermute(sent, "rows", swap))
    my_scale = lax.dynamic_slice(precision, ((height % across) * LANES,), (LANES,))[None, :]
    piece, copies = ((short, LANES), F32), ((deep, short, LANES), BF16)

    def over_feat(pieces):
        return lax.all_to_all(pieces, "feat", 0, 0)

    def over_z(pieces):
        return lax.all_to_all(pieces, "rows", 0, 0, axis_index_groups=levels)

    def rest(terms, more, first=False):
        message = sum_terms(over_feat(terms), more, first)
        pieces, sums = back_terms(over_feat(message), features, other, half, deep, first)
        return over_z(pieces), sums

    def apply(vectors):
        return rest(*image_terms(scale, features, other, vectors, n_feat))

    terms, other = first_image_terms(core, prior_noise, scale, features, other, n_feat)
    terms, perturbed, my_scale, group, core = lax.optimization_barrier(
        (terms, perturbed, my_scale, group, core)
    )
    terms, _ = rest(terms, perturbed, True)
    message, r0 = small_call(first_kernel, None, (terms,), (copies, piece))
    whole0 = over_z(message)

    terms, sums = apply((whole0,))
    message, r1, q0, scalars = small_call(
        second_kernel,
        group,
        (terms, sums, my_scale, r0),
        (copies, piece, piece, ((3, short, LANES), F32)),
    )
    whole1 = over_z(message)

    terms, sums = apply((whole1, whole0))
    (message,) = small_call(
        third_kernel,
        group,
        (terms, sums, my_scale, r0, r1, q0, scalars),
        (((deep, (short + 19) // 16 * 16, LANES), BF16),),
    )
    last = (over_z(message), whole0, whole1, prior_noise, scale)
    (mine,) = small_call(last_kernel, core, last, (((2, half, width), F32),))
    full = ((draws, width), F32)
    theirs = lax.ppermute(mine, "rows", swap)
    return tuple(small_call(join_kernel, core, (mine, theirs), (full, full)))


def solution(mesh):
    return jax.shard_map(
        shards,
        mesh=mesh,
        in_specs=(P("rows", "feat"), P("rows"), P(None, "rows"), P(None, "feat"), P("feat")),
        out_specs=(P(None, "feat"), P(None, "feat")),
        check_vma=False,
    )
```

```python
import functools
import math

import jax
import jax.numpy as jnp
from jax import lax
from jax.experimental import pallas as pl
from jax.experimental.pallas import tpu as pltpu
from jax.sharding import PartitionSpec as P

CORES = 2
LANES = 128
BLOCKS = 8
F32, BF16 = jnp.float32, jnp.bfloat16
MOST = 16 * 2**20
SCALARS = 16
LITTLE = 8 * 2**20
IN_VMEM = pl.BlockSpec(memory_space=pltpu.VMEM)
SMALL = pl.CostEstimate(flops=2**16, bytes_accessed=2**22, transcendentals=0)


def lane_index(rows):
    return lax.broadcasted_iota(jnp.int32, (rows, LANES), 1)


def column_to_row(column):
    rows = column.shape[0]
    at = lax.broadcasted_iota(jnp.int32, (rows, LANES), 0) == lane_index(rows)
    return jnp.sum(jnp.where(at, column, 0.0), axis=0, keepdims=True)


def row_to_column(row, rows, first=0):
    at = lax.broadcasted_iota(jnp.int32, (rows, LANES), 0) + first == lane_index(rows)
    return jnp.sum(jnp.where(at, row, 0.0), axis=1, keepdims=True)


def split(value):
    high = value.astype(BF16).astype(F32)
    return high, value - high


def assemble(pieces_ref, whole):
    tall = pieces_ref.shape[1]
    across = whole.shape[1] // LANES
    for m in range(pieces_ref.shape[0]):
        i, j = divmod(m, across)
        whole[pl.ds(i * tall, tall), pl.ds(j * LANES, LANES)] = pieces_ref[m].astype(F32)


def multiply_out(value, f_ref, store, wide, copies=None):
    chunks = f_ref.shape[0] // wide
    blocks = math.gcd(chunks, BLOCKS)
    per = chunks // blocks
    size = per * wide
    for k in range(blocks):
        if copies is not None:
            copies[k].wait()
        terms = lax.dot_general(
            value,
            f_ref[pl.ds(k * size, size)],
            (((1,), (1,)), ((), ())),
            preferred_element_type=F32,
        )
        for c in range(per):
            store(k * per + c, terms[:, c * wide : (c + 1) * wide])


def fetch(f_hbm, kept_ref, sems):
    count = sems.shape[0]
    size = f_hbm.shape[0] // count
    copies = []
    for k in range(count):
        at = pl.ds(k * size, size)
        copies.append(pltpu.make_async_copy(f_hbm.at[at], kept_ref.at[at], sems.at[k]))
        copies[k].start()
    return copies


def multiply_into(value, f_ref, pieces_ref, first, copies=None):
    def store(c, part):
        pieces_ref[first + c] = part.astype(BF16)

    multiply_out(value, f_ref, store, pieces_ref.shape[2], copies)


def own_image_kernel(core_ref, noise_ref, scale_ref, own_ref, pieces_ref, value_ref):
    draws = pieces_ref.shape[1]
    first = pl.multiple_of(core_ref[0] * draws, 8)
    value = (noise_ref[pl.ds(first, draws)] * lax.rsqrt(scale_ref[...])).astype(BF16)
    value_ref[...] = value
    multiply_into(value, own_ref, pieces_ref, 0)


def other_image_kernel(value_ref, half_ref, other_hbm, pieces_ref, kept_ref, sems):
    copies = fetch(other_hbm, kept_ref, sems)
    count = half_ref.shape[0]
    for c in range(count):
        pieces_ref[c] = half_ref[c]
    multiply_into(value_ref[...], kept_ref, pieces_ref, count, copies)


def image_kernel(count, scale_ref, own_ref, other_ref, *refs):
    vectors, (pieces_ref, sums_ref), wholes = (
        refs[:count],
        refs[count : count + 2],
        refs[count + 2 :],
    )
    for source, whole in zip(vectors, wholes):
        assemble(source, whole)
    value = wholes[0][...]
    direction = value.astype(BF16)
    multiply_into(direction, own_ref, pieces_ref, 0)
    multiply_into(direction, other_ref, pieces_ref, pieces_ref.shape[0] // CORES)
    sums = [value * value, value * value * scale_ref[...]]
    if count > 1:
        sums.append(value * wholes[1][...])
    lines = []
    for product in sums:
        column = jnp.sum(product, axis=1, keepdims=True)
        lines += [column_to_row(part) for part in split(column)]
    lines.append(jnp.zeros((SCALARS - len(lines), LANES), F32))
    sums_ref[...] = jnp.concatenate(lines, axis=0).astype(BF16)


def matmul_cost(draws, rows, width):
    return pl.CostEstimate(
        flops=2 * draws * rows * width, bytes_accessed=2 * rows * width, transcendentals=0
    )


def first_image_terms(core, noise, scale, own, other, n_feat):
    rows, width = own.shape
    draws = noise.shape[0] // CORES
    shape = (n_feat // CORES, draws, CORES * rows // n_feat)
    params = pltpu.CompilerParams(vmem_limit_bytes=MOST)
    half, value = pl.pallas_call(
        own_image_kernel,
        in_specs=[pl.BlockSpec(memory_space=pltpu.SMEM)] + [IN_VMEM] * 3,
        out_specs=[IN_VMEM] * 2,
        out_shape=[
            jax.ShapeDtypeStruct(shape, BF16),
            jax.ShapeDtypeStruct((draws, width), BF16),
        ],
        compiler_params=params,
        cost_estimate=matmul_cost(draws, rows, width),
    )(core, noise, scale, own)
    terms, other = pl.pallas_call(
        other_image_kernel,
        in_specs=[IN_VMEM] * 2 + [pl.BlockSpec(memory_space=pl.ANY)],
        out_specs=[IN_VMEM] * 2,
        out_shape=[
            jax.ShapeDtypeStruct((n_feat,) + shape[1:], BF16),
            jax.ShapeDtypeStruct((rows, width), BF16),
        ],
        scratch_shapes=[pltpu.SemaphoreType.DMA((math.gcd(shape[0], BLOCKS),))],
        compiler_params=params,
        cost_estimate=matmul_cost(draws, rows, width),
    )(value, half, other)
    return terms, other


def image_terms(scale, own, other, vectors, n_feat):
    rows, width = own.shape
    draws = vectors[0].size // width
    count = len(vectors)
    return pl.pallas_call(
        functools.partial(image_kernel, count),
        in_specs=[IN_VMEM] * (3 + count),
        out_specs=[IN_VMEM] * 2,
        out_shape=[
            jax.ShapeDtypeStruct((n_feat, draws, CORES * rows // n_feat), BF16),
            jax.ShapeDtypeStruct((SCALARS, LANES), BF16),
        ],
        scratch_shapes=[pltpu.VMEM((draws, width), F32)] * count,
        compiler_params=pltpu.CompilerParams(vmem_limit_bytes=MOST),
        cost_estimate=matmul_cost(draws, CORES * rows, width),
    )(scale, own, other, *vectors)


def sum_kernel(first, terms_ref, more_ref, message_ref):
    count, tall, wide = terms_ref.shape
    total = terms_ref[0].astype(F32)
    for k in range(1, count):
        total = total + terms_ref[k].astype(F32)
    if first:
        total = more_ref[...] - total
    total = total.astype(BF16)
    for k in range(count):
        for b in range(wide // LANES):
            at = pl.ds(b * tall, tall)
            message_ref[k, at] = total[:, b * LANES : (b + 1) * LANES]
        if not first:
            message_ref[k, pl.ds(wide // LANES * tall, SCALARS)] = more_ref[...]


def sum_terms(terms, more, first):
    count, tall, wide = terms.shape
    return pl.pallas_call(
        functools.partial(sum_kernel, first),
        out_shape=jax.ShapeDtypeStruct(
            (count, tall * wide // LANES + (0 if first else SCALARS), LANES), BF16
        ),
        compiler_params=pltpu.CompilerParams(vmem_limit_bytes=LITTLE),
        cost_estimate=pl.CostEstimate(
            flops=terms.size, bytes_accessed=4 * terms.size, transcendentals=0
        ),
    )(terms, more)


def back_kernel(first, message_ref, own_ref, other_ref, pieces_ref, sums_ref, errors):
    count = message_ref.shape[0]
    draws, wide = errors.shape[0], errors.shape[1] // count
    rows = own_ref.shape[0]
    for c in range(count):
        for b in range(wide // LANES):
            errors[:, pl.ds(c * wide + b * LANES, LANES)] = message_ref[
                c, pl.ds(b * draws, draws)
            ]
    total = jnp.dot(errors[:, pl.ds(0, rows)], own_ref[...], preferred_element_type=F32)
    total = total + jnp.dot(
        errors[:, pl.ds(rows, rows)], other_ref[...], preferred_element_type=F32
    )
    across = own_ref.shape[1] // LANES
    short = sums_ref.shape[1]
    if first:
        sums_ref[...] = jnp.zeros(sums_ref.shape, F32)
        for m in range(pieces_ref.shape[0]):
            i, j = divmod(m, across)
            piece = total[i * short : (i + 1) * short, j * LANES : (j + 1) * LANES]
            pieces_ref[m] = piece.astype(BF16)
        return
    squares = jnp.zeros((draws, LANES), F32)
    for at in range(0, errors.shape[1], LANES):
        part = errors[:, pl.ds(at, LANES)].astype(F32)
        squares = squares + part * part
    high, low = split(jnp.sum(squares, axis=1, keepdims=True))
    packed = jnp.zeros((SCALARS, LANES), F32)
    for k in range(count):
        part = message_ref[k, pl.ds(wide // LANES * draws, SCALARS)]
        packed = packed + part.astype(F32)
    lane = lane_index(short)
    empty = jnp.zeros((pieces_ref.shape[1] - short - 2, LANES), F32)
    for i in range(sums_ref.shape[0]):
        mine = slice(i * short, (i + 1) * short)
        plain = jnp.zeros((short, LANES), F32)
        for k in range(3):
            line = packed[2 * k : 2 * k + 1] + packed[2 * k + 1 : 2 * k + 2]
            plain = jnp.where(lane == k, row_to_column(line, short, i * short), plain)
        sums_ref[i] = plain
        extra = [column_to_row(high[mine]), column_to_row(low[mine]), empty]
        for j in range(across):
            piece = total[mine, j * LANES : (j + 1) * LANES]
            pieces_ref[i * across + j] = jnp.concatenate([piece] + extra, axis=0).astype(BF16)


def back_terms(message, own, other, draws, pieces, first):
    rows, width = own.shape
    short = draws * width // LANES // pieces
    return pl.pallas_call(
        functools.partial(back_kernel, first),
        in_specs=[IN_VMEM] * 3,
        out_specs=[IN_VMEM] * 2,
        out_shape=[
            jax.ShapeDtypeStruct(
                (pieces, short if first else (short + 17) // 16 * 16, LANES), BF16
            ),
            jax.ShapeDtypeStruct((draws // short, short, LANES), F32),
        ],
        scratch_shapes=[pltpu.VMEM((draws, CORES * rows), BF16)],
        compiler_params=pltpu.CompilerParams(vmem_limit_bytes=MOST),
        cost_estimate=matmul_cost(draws, CORES * rows, width),
    )(message, own, other)


def pick(sums_ref, group_ref, rows):
    mine = sums_ref[group_ref[0]]
    lane = lane_index(rows)
    return [
        jnp.sum(jnp.where(lane == k, mine, 0.0), axis=1, keepdims=True) for k in range(3)
    ]


def add_up(terms_ref):
    total = terms_ref[0].astype(F32)
    for k in range(1, terms_ref.shape[0]):
        total = total + terms_ref[k].astype(F32)
    return total


def received(terms_ref, rows):
    total = add_up(terms_ref)
    norm = row_to_column(total[rows : rows + 1] + total[rows + 1 : rows + 2], rows)
    return total[:rows], norm


def to_all(message_ref, value):
    value = value.astype(BF16)
    for k in range(message_ref.shape[0]):
        message_ref[k] = value


def first_kernel(terms_ref, message_ref, r0_ref):
    r0 = add_up(terms_ref)
    r0_ref[...] = r0
    to_all(message_ref, r0)


def second_kernel(
    group_ref, terms_ref, sums_ref, scale_ref, r0_ref, message_ref, r1_ref, q0_ref, scalar_ref
):
    rows = r0_ref.shape[0]
    product, norm = received(terms_ref, rows)
    rr, weighted, _ = pick(sums_ref, group_ref, rows)
    curve = norm + weighted
    alpha = rr / curve
    q0 = product + scale_ref[...] * r0_ref[...]
    r1 = r0_ref[...] - alpha * q0
    r1_ref[...] = r1
    q0_ref[...] = q0
    scalar_ref[0] = jnp.broadcast_to(rr, (rows, LANES))
    scalar_ref[1] = jnp.broadcast_to(alpha, (rows, LANES))
    scalar_ref[2] = jnp.broadcast_to(curve, (rows, LANES))
    to_all(message_ref, r1)


def third_kernel(
    group_ref, terms_ref, sums_ref, scale_ref, r0_ref, r1_ref, q0_ref, scalar_ref, message_ref
):
    rows = r0_ref.shape[0]
    product, norm = received(terms_ref, rows)
    new, weighted, cross = pick(sums_ref, group_ref, rows)
    rr, alpha0, curve0 = (scalar_ref[k][:, :1] for k in range(3))
    beta = new / rr
    mixed = (cross - new) / alpha0
    curve = norm + weighted + 2.0 * beta * mixed + beta * beta * curve0
    alpha = new / curve
    r1 = r1_ref[...]
    applied = product + scale_ref[...] * r1 + beta * q0_ref[...]
    parts = [r1 - alpha * applied]
    for scalar in (alpha0 + alpha * beta, alpha):
        parts += [column_to_row(part) for part in split(scalar)]
    short = message_ref.shape[1] - rows - 4
    if short > 0:
        parts.append(jnp.zeros((short, LANES), F32))
    to_all(message_ref, jnp.concatenate(parts, axis=0))


def small_call(kernel, group, operands, outs):
    specs = [IN_VMEM] * len(operands)
    if group is not None:
        specs = [pl.BlockSpec(memory_space=pltpu.SMEM)] + specs
        operands = (group,) + operands
    return pl.pallas_call(
        kernel,
        in_specs=specs,
        out_specs=[IN_VMEM] * len(outs),
        out_shape=[jax.ShapeDtypeStruct(shape, kind) for shape, kind in outs],
        compiler_params=pltpu.CompilerParams(vmem_limit_bytes=LITTLE),
        cost_estimate=SMALL,
    )(*operands)


def last_kernel(core_ref, pieces_ref, whole0_ref, whole1_ref, noise_ref, scale_ref, out_ref):
    tall = whole0_ref.shape[1]
    draws = out_ref.shape[1]
    across = out_ref.shape[2] // LANES
    first = pl.multiple_of(core_ref[0] * draws, 8)
    out_ref[0] = noise_ref[pl.ds(first, draws)] * lax.rsqrt(scale_ref[...])
    for m in range(pieces_ref.shape[0]):
        i, j = divmod(m, across)
        at = (pl.ds(i * tall, tall), pl.ds(j * LANES, LANES))
        piece = pieces_ref[m].astype(F32)
        part0, part1 = (
            row_to_column(piece[k : k + 1] + piece[k + 1 : k + 2], tall)
            for k in (tall, tall + 2)
        )
        moved = part0 * whole0_ref[m].astype(F32) + part1 * whole1_ref[m].astype(F32)
        out_ref[(0,) + at] = out_ref[(0,) + at] + moved
        out_ref[(1,) + at] = piece[:tall]


def join_kernel(core_ref, own_ref, other_ref, sampled_ref, residual_ref):
    draws = own_ref.shape[1]
    for core, source in ((core_ref[0], own_ref), (1 - core_ref[0], other_ref)):
        at = pl.ds(pl.multiple_of(core * draws, 8), draws)
        sampled_ref[at] = source[0]
        residual_ref[at] = source[1]


def shards(features, targets, target_noise, prior_noise, precision):
    n_feat = lax.axis_size("feat")
    n_rows = lax.axis_size("rows")
    draws, width = prior_noise.shape
    rows = features.shape[0]
    half = draws // CORES
    chunks = n_feat // CORES
    wide = rows // chunks
    deep = n_rows // CORES
    across = width // LANES
    short = half * across // deep

    levels = [[CORES * z + core for z in range(deep)] for core in range(CORES)]
    swap = [(i, i ^ 1) for i in range(n_rows)]
    other = lax.ppermute(features, "rows", swap)

    scale = precision[None, :]
    line = lax.axis_index("rows").astype(jnp.int32)
    height = line // CORES
    core = (line % CORES).reshape(1)
    group = (height // across).reshape(1)
    place = lax.axis_index("feat")
    first_row = (place % chunks) * wide
    my_targets = lax.dynamic_slice(targets, (first_row,), (wide,))[None, :]
    kept, sent = (
        my_targets + lax.dynamic_slice(target_noise, (side * half, first_row), (half, wide))
        for side in (core[0], 1 - core[0])
    )
    perturbed = jnp.where(place < chunks, kept, lax.ppermute(sent, "rows", swap))
    my_scale = lax.dynamic_slice(precision, ((height % across) * LANES,), (LANES,))[None, :]
    piece, copies = ((short, LANES), F32), ((deep, short, LANES), BF16)

    def over_feat(pieces):
        return lax.all_to_all(pieces, "feat", 0, 0)

    def over_z(pieces):
        return lax.all_to_all(pieces, "rows", 0, 0, axis_index_groups=levels)

    def rest(terms, more, first=False):
        message = sum_terms(over_feat(terms), more, first)
        pieces, sums = back_terms(over_feat(message), features, other, half, deep, first)
        return over_z(pieces), sums

    def apply(vectors):
        return rest(*image_terms(scale, features, other, vectors, n_feat))

    terms, other = first_image_terms(core, prior_noise, scale, features, other, n_feat)
    terms, perturbed, my_scale, group, core = lax.optimization_barrier(
        (terms, perturbed, my_scale, group, core)
    )
    terms, _ = rest(terms, perturbed, True)
    message, r0 = small_call(first_kernel, None, (terms,), (copies, piece))
    whole0 = over_z(message)

    terms, sums = apply((whole0,))
    message, r1, q0, scalars = small_call(
        second_kernel,
        group,
        (terms, sums, my_scale, r0),
        (copies, piece, piece, ((3, short, LANES), F32)),
    )
    whole1 = over_z(message)

    terms, sums = apply((whole1, whole0))
    (message,) = small_call(
        third_kernel,
        group,
        (terms, sums, my_scale, r0, r1, q0, scalars),
        (((deep, (short + 19) // 16 * 16, LANES), BF16),),
    )
    last = (over_z(message), whole0, whole1, prior_noise, scale)
    (mine,) = small_call(last_kernel, core, last, (((2, half, width), F32),))
    full = ((draws, width), F32)
    theirs = lax.ppermute(mine, "rows", swap)
    return tuple(small_call(join_kernel, core, (mine, theirs), (full, full)))


def solution(mesh):
    return jax.shard_map(
        shards,
        mesh=mesh,
        in_specs=(P("rows", "feat"), P("rows"), P(None, "rows"), P(None, "feat"), P("feat")),
        out_specs=(P(None, "feat"), P(None, "feat")),
        check_vma=False,
    )
```

```python
import functools
import math

import jax
import jax.numpy as jnp
from jax import lax
from jax.experimental import pallas as pl
from jax.experimental.pallas import tpu as pltpu
from jax.sharding import PartitionSpec as P

CORES = 2
LANES = 128
BLOCKS = 8
PARTS = 4
F32, BF16 = jnp.float32, jnp.bfloat16
MOST = 16 * 2**20
SCALARS = 16
LITTLE = 8 * 2**20
IN_VMEM = pl.BlockSpec(memory_space=pltpu.VMEM)
SMALL = pl.CostEstimate(flops=2**16, bytes_accessed=2**22, transcendentals=0)


def lane_index(rows):
    return lax.broadcasted_iota(jnp.int32, (rows, LANES), 1)


def column_to_row(column):
    rows = column.shape[0]
    at = lax.broadcasted_iota(jnp.int32, (rows, LANES), 0) == lane_index(rows)
    return jnp.sum(jnp.where(at, column, 0.0), axis=0, keepdims=True)


def row_to_column(row, rows, first=0):
    at = lax.broadcasted_iota(jnp.int32, (rows, LANES), 0) + first == lane_index(rows)
    return jnp.sum(jnp.where(at, row, 0.0), axis=1, keepdims=True)


def split(value):
    high = value.astype(BF16).astype(F32)
    return high, value - high


def assemble(pieces_ref, whole):
    tall = pieces_ref.shape[1]
    across = whole.shape[1] // LANES
    for m in range(pieces_ref.shape[0]):
        i, j = divmod(m, across)
        whole[pl.ds(i * tall, tall), pl.ds(j * LANES, LANES)] = pieces_ref[m].astype(F32)


def multiply_out(value, f_ref, store, wide, copies=None):
    chunks = f_ref.shape[0] // wide
    blocks = math.gcd(chunks, BLOCKS if copies is None else PARTS)
    per = chunks // blocks
    size = per * wide
    for k in range(blocks):
        if copies is not None:
            copies[k].wait()
        terms = lax.dot_general(
            value,
            f_ref[pl.ds(k * size, size)],
            (((1,), (1,)), ((), ())),
            preferred_element_type=F32,
        )
        for c in range(per):
            store(k * per + c, terms[:, c * wide : (c + 1) * wide])


def fetch(f_hbm, kept_ref, sems):
    count = sems.shape[0]
    size = f_hbm.shape[0] // count
    copies = []
    for k in range(count):
        at = pl.ds(k * size, size)
        copies.append(pltpu.make_async_copy(f_hbm.at[at], kept_ref.at[at], sems.at[k]))
        copies[k].start()
    return copies


def multiply_into(value, f_ref, pieces_ref, first, copies=None):
    def store(c, part):
        pieces_ref[first + c] = part.astype(BF16)

    multiply_out(value, f_ref, store, pieces_ref.shape[2], copies)


def own_image_kernel(core_ref, noise_ref, scale_ref, own_ref, pieces_ref, value_ref):
    draws = pieces_ref.shape[1]
    first = pl.multiple_of(core_ref[0] * draws, 8)
    value = (noise_ref[pl.ds(first, draws)] * lax.rsqrt(scale_ref[...])).astype(BF16)
    value_ref[...] = value
    multiply_into(value, own_ref, pieces_ref, 0)


def other_image_kernel(value_ref, half_ref, other_hbm, pieces_ref, kept_ref, sems):
    copies = fetch(other_hbm, kept_ref, sems)
    count = half_ref.shape[0]
    for c in range(count):
        pieces_ref[c] = half_ref[c]
    multiply_into(value_ref[...], kept_ref, pieces_ref, count, copies)


def image_kernel(count, scale_ref, own_ref, other_ref, *refs):
    vectors, (pieces_ref, sums_ref), wholes = (
        refs[:count],
        refs[count : count + 2],
        refs[count + 2 :],
    )
    for source, whole in zip(vectors, wholes):
        assemble(source, whole)
    value = wholes[0][...]
    direction = value.astype(BF16)
    multiply_into(direction, own_ref, pieces_ref, 0)
    multiply_into(direction, other_ref, pieces_ref, pieces_ref.shape[0] // CORES)
    sums = [value * value, value * value * scale_ref[...]]
    if count > 1:
        sums.append(value * wholes[1][...])
    lines = []
    for product in sums:
        column = jnp.sum(product, axis=1, keepdims=True)
        lines += [column_to_row(part) for part in split(column)]
    lines.append(jnp.zeros((SCALARS - len(lines), LANES), F32))
    sums_ref[...] = jnp.concatenate(lines, axis=0).astype(BF16)


def matmul_cost(draws, rows, width):
    return pl.CostEstimate(
        flops=2 * draws * rows * width, bytes_accessed=2 * rows * width, transcendentals=0
    )


def first_image_terms(core, noise, scale, own, other, n_feat):
    rows, width = own.shape
    draws = noise.shape[0] // CORES
    shape = (n_feat // CORES, draws, CORES * rows // n_feat)
    params = pltpu.CompilerParams(vmem_limit_bytes=MOST)
    half, value = pl.pallas_call(
        own_image_kernel,
        in_specs=[pl.BlockSpec(memory_space=pltpu.SMEM)] + [IN_VMEM] * 3,
        out_specs=[IN_VMEM] * 2,
        out_shape=[
            jax.ShapeDtypeStruct(shape, BF16),
            jax.ShapeDtypeStruct((draws, width), BF16),
        ],
        compiler_params=params,
        cost_estimate=matmul_cost(draws, rows, width),
    )(core, noise, scale, own)
    terms, other = pl.pallas_call(
        other_image_kernel,
        in_specs=[IN_VMEM] * 2 + [pl.BlockSpec(memory_space=pl.ANY)],
        out_specs=[IN_VMEM] * 2,
        out_shape=[
            jax.ShapeDtypeStruct((n_feat,) + shape[1:], BF16),
            jax.ShapeDtypeStruct((rows, width), BF16),
        ],
        scratch_shapes=[pltpu.SemaphoreType.DMA((math.gcd(shape[0], PARTS),))],
        compiler_params=params,
        cost_estimate=matmul_cost(draws, rows, width),
    )(value, half, other)
    return terms, other


def image_terms(scale, own, other, vectors, n_feat):
    rows, width = own.shape
    draws = vectors[0].size // width
    count = len(vectors)
    return pl.pallas_call(
        functools.partial(image_kernel, count),
        in_specs=[IN_VMEM] * (3 + count),
        out_specs=[IN_VMEM] * 2,
        out_shape=[
            jax.ShapeDtypeStruct((n_feat, draws, CORES * rows // n_feat), BF16),
            jax.ShapeDtypeStruct((SCALARS, LANES), BF16),
        ],
        scratch_shapes=[pltpu.VMEM((draws, width), F32)] * count,
        compiler_params=pltpu.CompilerParams(vmem_limit_bytes=MOST),
        cost_estimate=matmul_cost(draws, CORES * rows, width),
    )(scale, own, other, *vectors)


def sum_kernel(first, *refs):
    terms_ref, message_ref = refs[0], refs[-1]
    count, tall, wide = terms_ref.shape
    total = terms_ref[0].astype(F32)
    for k in range(1, count):
        total = total + terms_ref[k].astype(F32)
    if first:
        kept_ref, received_ref, core_ref, far_ref = refs[1:5]
        mine = pl.ds(pl.multiple_of(core_ref[0] * tall, 8), tall)
        is_kept = jnp.full((tall, wide), far_ref[0]) == 0
        total = jnp.where(is_kept, kept_ref[mine], received_ref[mine]) - total
    else:
        more_ref = refs[1]
    total = total.astype(BF16)
    for k in range(count):
        for b in range(wide // LANES):
            at = pl.ds(b * tall, tall)
            message_ref[k, at] = total[:, b * LANES : (b + 1) * LANES]
        if not first:
            message_ref[k, pl.ds(wide // LANES * tall, SCALARS)] = more_ref[...]


def sum_terms(terms, more):
    first = len(more) > 1
    count, tall, wide = terms.shape
    specs = [IN_VMEM] * (1 + len(more))
    if first:
        specs[-2:] = [pl.BlockSpec(memory_space=pltpu.SMEM)] * 2
    return pl.pallas_call(
        functools.partial(sum_kernel, first),
        in_specs=specs,
        out_specs=IN_VMEM,
        out_shape=jax.ShapeDtypeStruct(
            (count, tall * wide // LANES + (0 if first else SCALARS), LANES), BF16
        ),
        compiler_params=pltpu.CompilerParams(vmem_limit_bytes=LITTLE),
        cost_estimate=pl.CostEstimate(
            flops=terms.size, bytes_accessed=4 * terms.size, transcendentals=0
        ),
    )(terms, *more)


def back_kernel(first, message_ref, own_ref, other_ref, pieces_ref, sums_ref, errors):
    count = message_ref.shape[0]
    draws, wide = errors.shape[0], errors.shape[1] // count
    rows = own_ref.shape[0]
    for c in range(count):
        for b in range(wide // LANES):
            errors[:, pl.ds(c * wide + b * LANES, LANES)] = message_ref[
                c, pl.ds(b * draws, draws)
            ]
    total = jnp.dot(errors[:, pl.ds(0, rows)], own_ref[...], preferred_element_type=F32)
    total = total + jnp.dot(
        errors[:, pl.ds(rows, rows)], other_ref[...], preferred_element_type=F32
    )
    across = own_ref.shape[1] // LANES
    short = sums_ref.shape[1]
    if first:
        sums_ref[...] = jnp.zeros(sums_ref.shape, F32)
        for m in range(pieces_ref.shape[0]):
            i, j = divmod(m, across)
            piece = total[i * short : (i + 1) * short, j * LANES : (j + 1) * LANES]
            pieces_ref[m] = piece.astype(BF16)
        return
    squares = jnp.zeros((draws, LANES), F32)
    for at in range(0, errors.shape[1], LANES):
        part = errors[:, pl.ds(at, LANES)].astype(F32)
        squares = squares + part * part
    high, low = split(jnp.sum(squares, axis=1, keepdims=True))
    packed = jnp.zeros((SCALARS, LANES), F32)
    for k in range(count):
        part = message_ref[k, pl.ds(wide // LANES * draws, SCALARS)]
        packed = packed + part.astype(F32)
    lane = lane_index(short)
    empty = jnp.zeros((pieces_ref.shape[1] - short - 2, LANES), F32)
    for i in range(sums_ref.shape[0]):
        mine = slice(i * short, (i + 1) * short)
        plain = jnp.zeros((short, LANES), F32)
        for k in range(3):
            line = packed[2 * k : 2 * k + 1] + packed[2 * k + 1 : 2 * k + 2]
            plain = jnp.where(lane == k, row_to_column(line, short, i * short), plain)
        sums_ref[i] = plain
        extra = [column_to_row(high[mine]), column_to_row(low[mine]), empty]
        for j in range(across):
            piece = total[mine, j * LANES : (j + 1) * LANES]
            pieces_ref[i * across + j] = jnp.concatenate([piece] + extra, axis=0).astype(BF16)


def back_terms(message, own, other, draws, pieces, first):
    rows, width = own.shape
    short = draws * width // LANES // pieces
    return pl.pallas_call(
        functools.partial(back_kernel, first),
        in_specs=[IN_VMEM] * 3,
        out_specs=[IN_VMEM] * 2,
        out_shape=[
            jax.ShapeDtypeStruct(
                (pieces, short if first else (short + 17) // 16 * 16, LANES), BF16
            ),
            jax.ShapeDtypeStruct((draws // short, short, LANES), F32),
        ],
        scratch_shapes=[pltpu.VMEM((draws, CORES * rows), BF16)],
        compiler_params=pltpu.CompilerParams(vmem_limit_bytes=MOST),
        cost_estimate=matmul_cost(draws, CORES * rows, width),
    )(message, own, other)


def pick(sums_ref, group_ref, rows):
    mine = sums_ref[group_ref[0]]
    lane = lane_index(rows)
    return [
        jnp.sum(jnp.where(lane == k, mine, 0.0), axis=1, keepdims=True) for k in range(3)
    ]


def add_up(terms_ref):
    total = terms_ref[0].astype(F32)
    for k in range(1, terms_ref.shape[0]):
        total = total + terms_ref[k].astype(F32)
    return total


def received(terms_ref, rows):
    total = add_up(terms_ref)
    norm = row_to_column(total[rows : rows + 1] + total[rows + 1 : rows + 2], rows)
    return total[:rows], norm


def to_all(message_ref, value):
    value = value.astype(BF16)
    for k in range(message_ref.shape[0]):
        message_ref[k] = value


def first_kernel(terms_ref, message_ref, r0_ref):
    r0 = add_up(terms_ref)
    r0_ref[...] = r0
    to_all(message_ref, r0)


def second_kernel(
    group_ref, terms_ref, sums_ref, scale_ref, r0_ref, message_ref, r1_ref, q0_ref, scalar_ref
):
    rows = r0_ref.shape[0]
    product, norm = received(terms_ref, rows)
    rr, weighted, _ = pick(sums_ref, group_ref, rows)
    curve = norm + weighted
    alpha = rr / curve
    q0 = product + scale_ref[...] * r0_ref[...]
    r1 = r0_ref[...] - alpha * q0
    r1_ref[...] = r1
    q0_ref[...] = q0
    scalar_ref[0] = jnp.broadcast_to(rr, (rows, LANES))
    scalar_ref[1] = jnp.broadcast_to(alpha, (rows, LANES))
    scalar_ref[2] = jnp.broadcast_to(curve, (rows, LANES))
    to_all(message_ref, r1)


def third_kernel(
    group_ref, terms_ref, sums_ref, scale_ref, r0_ref, r1_ref, q0_ref, scalar_ref, message_ref
):
    rows = r0_ref.shape[0]
    product, norm = received(terms_ref, rows)
    new, weighted, cross = pick(sums_ref, group_ref, rows)
    rr, alpha0, curve0 = (scalar_ref[k][:, :1] for k in range(3))
    beta = new / rr
    mixed = (cross - new) / alpha0
    curve = norm + weighted + 2.0 * beta * mixed + beta * beta * curve0
    alpha = new / curve
    r1 = r1_ref[...]
    applied = product + scale_ref[...] * r1 + beta * q0_ref[...]
    parts = [r1 - alpha * applied]
    for scalar in (alpha0 + alpha * beta, alpha):
        parts += [column_to_row(part) for part in split(scalar)]
    short = message_ref.shape[1] - rows - 4
    if short > 0:
        parts.append(jnp.zeros((short, LANES), F32))
    to_all(message_ref, jnp.concatenate(parts, axis=0))


def small_call(kernel, group, operands, outs):
    specs = [IN_VMEM] * len(operands)
    if group is not None:
        specs = [pl.BlockSpec(memory_space=pltpu.SMEM)] + specs
        operands = (group,) + operands
    return pl.pallas_call(
        kernel,
        in_specs=specs,
        out_specs=[IN_VMEM] * len(outs),
        out_shape=[jax.ShapeDtypeStruct(shape, kind) for shape, kind in outs],
        compiler_params=pltpu.CompilerParams(vmem_limit_bytes=LITTLE),
        cost_estimate=SMALL,
    )(*operands)


def last_kernel(core_ref, pieces_ref, whole0_ref, whole1_ref, noise_ref, scale_ref, out_ref):
    tall = whole0_ref.shape[1]
    draws = out_ref.shape[1]
    across = out_ref.shape[2] // LANES
    first = pl.multiple_of(core_ref[0] * draws, 8)
    out_ref[0] = noise_ref[pl.ds(first, draws)] * lax.rsqrt(scale_ref[...])
    for m in range(pieces_ref.shape[0]):
        i, j = divmod(m, across)
        at = (pl.ds(i * tall, tall), pl.ds(j * LANES, LANES))
        piece = pieces_ref[m].astype(F32)
        part0, part1 = (
            row_to_column(piece[k : k + 1] + piece[k + 1 : k + 2], tall)
            for k in (tall, tall + 2)
        )
        moved = part0 * whole0_ref[m].astype(F32) + part1 * whole1_ref[m].astype(F32)
        out_ref[(0,) + at] = out_ref[(0,) + at] + moved
        out_ref[(1,) + at] = piece[:tall]


def join_kernel(core_ref, own_ref, other_ref, sampled_ref, residual_ref):
    draws = own_ref.shape[1]
    for core, source in ((core_ref[0], own_ref), (1 - core_ref[0], other_ref)):
        at = pl.ds(pl.multiple_of(core * draws, 8), draws)
        sampled_ref[at] = source[0]
        residual_ref[at] = source[1]


def shards(features, targets, target_noise, prior_noise, precision):
    n_feat = lax.axis_size("feat")
    n_rows = lax.axis_size("rows")
    draws, width = prior_noise.shape
    rows = features.shape[0]
    half = draws // CORES
    chunks = n_feat // CORES
    wide = rows // chunks
    deep = n_rows // CORES
    across = width // LANES
    short = half * across // deep

    levels = [[CORES * z + core for z in range(deep)] for core in range(CORES)]
    swap = [(i, i ^ 1) for i in range(n_rows)]
    other = lax.ppermute(features, "rows", swap)

    scale = precision[None, :]
    line = lax.axis_index("rows").astype(jnp.int32)
    height = line // CORES
    core = (line % CORES).reshape(1)
    group = (height // across).reshape(1)
    place = lax.axis_index("feat")
    first_row = (place % chunks) * wide
    perturbed = lax.dynamic_slice(targets, (first_row,), (wide,))[None, :] + lax.dynamic_slice(
        target_noise, (0, first_row), (draws, wide)
    )
    received = lax.ppermute(perturbed, "rows", swap)
    far = (place >= chunks).astype(jnp.int32).reshape(1)
    my_scale = lax.dynamic_slice(precision, ((height % across) * LANES,), (LANES,))[None, :]
    piece, copies = ((short, LANES), F32), ((deep, short, LANES), BF16)

    def over_feat(pieces):
        return lax.all_to_all(pieces, "feat", 0, 0)

    def over_z(pieces):
        return lax.all_to_all(pieces, "rows", 0, 0, axis_index_groups=levels)

    def rest(terms, more, first=False):
        message = sum_terms(over_feat(terms), more)
        pieces, sums = back_terms(over_feat(message), features, other, half, deep, first)
        return over_z(pieces), sums

    def apply(vectors):
        terms, sums = image_terms(scale, features, other, vectors, n_feat)
        return rest(terms, (sums,))

    terms, other = first_image_terms(core, prior_noise, scale, features, other, n_feat)
    terms, perturbed, received, far, my_scale, group, core = lax.optimization_barrier(
        (terms, perturbed, received, far, my_scale, group, core)
    )
    terms, _ = rest(terms, (perturbed, received, core, far), True)
    message, r0 = small_call(first_kernel, None, (terms,), (copies, piece))
    whole0 = over_z(message)

    terms, sums = apply((whole0,))
    message, r1, q0, scalars = small_call(
        second_kernel,
        group,
        (terms, sums, my_scale, r0),
        (copies, piece, piece, ((3, short, LANES), F32)),
    )
    whole1 = over_z(message)

    terms, sums = apply((whole1, whole0))
    (message,) = small_call(
        third_kernel,
        group,
        (terms, sums, my_scale, r0, r1, q0, scalars),
        (((deep, (short + 19) // 16 * 16, LANES), BF16),),
    )
    last = (over_z(message), whole0, whole1, prior_noise, scale)
    (mine,) = small_call(last_kernel, core, last, (((2, half, width), F32),))
    full = ((draws, width), F32)
    theirs = lax.ppermute(mine, "rows", swap)
    return tuple(small_call(join_kernel, core, (mine, theirs), (full, full)))


def solution(mesh):
    return jax.shard_map(
        shards,
        mesh=mesh,
        in_specs=(P("rows", "feat"), P("rows"), P(None, "rows"), P(None, "feat"), P("feat")),
        out_specs=(P(None, "feat"), P(None, "feat")),
        check_vma=False,
    )
```
